32 devices in a mesh: seq: 2 (over x), sect: 4 (over y, core), mp: 4 (over z).
Axes of the slice: x: 2, y: 2, z: 4, core: 2. Of those that a mesh axis runs over, the one named last changes fastest.
Arguments:
- enc_query: bfloat16 [4, 256, 2048], P('sect', 'seq', 'mp'), may hold values from -15 to 15
- enc_keys: bfloat16 [4, 256, 2048], P('sect', 'seq', 'mp'), may hold values from -6 to 6
- enc_values: bfloat16 [4, 256, 2048], P('sect', 'seq', 'mp'), may hold values from -6 to 6
- enc_lengths: int32 [4], replicated, may hold values from 192 to 256, as said below
- cross_keys: bfloat16 [4, 256, 2048], P('sect', 'seq', 'mp'), may hold values from -6 to 6
- cross_values: bfloat16 [4, 256, 2048], P('sect', 'seq', 'mp'), may hold values from -6 to 6
- cross_query: bfloat16 [128, 4, 512], P('seq', 'mp', 'sect'), may hold values from -15 to 15
- dec_query: bfloat16 [128, 4, 512], P('seq', 'mp', 'sect'), may hold values from -15 to 15
- dec_keys: bfloat16 [128, 4, 512], P('seq', 'mp', 'sect'), may hold values from -6 to 6
- dec_values: bfloat16 [128, 4, 512], P('seq', 'mp', 'sect'), may hold values from -6 to 6
- cross_out_weight: bfloat16 [4, 512, 4096], P('mp', 'sect'), may hold values from -0.125 to 0.125
- dec_hidden: bfloat16 [128, 4096], P('seq', ('sect', 'mp')), may hold values from -6 to 6
Outputs:
- enc_context: bfloat16 [4, 256, 2048], P('sect', 'seq', 'mp')
- self_context: bfloat16 [128, 4, 512], P('seq', 'mp', 'sect')
- decoded: bfloat16 [128, 4096], P('seq', ('sect', 'mp'))
The draws below stay inside these ranges and needn't reach their ends.
Inputs may be any that keep to these rules, and one draw needn't show every extreme that they name: `enc_lengths`: at least one micro-batch has all 256 positions valid.
All inputs are finite; a program needn't handle non-finite values.
Results may differ from the reference program's by a relative error of at most 0.012.
Values may be sent and summed in bfloat16 or wider, within the bound.
A program may use at most 128 MiB of HBM per device.

```python
import jax
import jax.numpy as jnp
from jax import lax

HEAD_DIM = 64
D = 4096
WIDTH = 2048
BATCHES = 4
L_ENC = 256
L_DEC = 128
GROUPS = 4
GROUP_W = 512


def draw_enc_query(key, part):
    key = jax.random.fold_in(key, 1)
    base = 2.5 * jax.random.truncated_normal(key, -6.0, 6.0, (BATCHES, L_ENC, WIDTH))
    return base.astype(jnp.bfloat16)


def draw_enc_keys(key, part):
    key = jax.random.fold_in(key, 2)
    base = jax.random.truncated_normal(key, -6.0, 6.0, (BATCHES, L_ENC, WIDTH))
    return base.astype(jnp.bfloat16)


def draw_enc_lengths(key, part):
    key = jax.random.fold_in(key, 3)
    length_key, full_key = jax.random.split(key)
    lengths = jax.random.randint(length_key, (BATCHES,), 3 * L_ENC // 4, L_ENC + 1)
    full_index = jax.random.randint(full_key, (), 0, BATCHES)
    return jnp.where(jnp.arange(BATCHES) == full_index, L_ENC, lengths).astype(jnp.int32)


def draw_cross_keys(key, part):
    key = jax.random.fold_in(key, 4)
    base = jax.random.truncated_normal(key, -6.0, 6.0, (BATCHES, L_ENC, WIDTH))
    return base.astype(jnp.bfloat16)


def draw_cross_query(key, part):
    key = jax.random.fold_in(key, 5)
    base = 2.5 * jax.random.truncated_normal(key, -6.0, 6.0, (L_DEC, WIDTH))
    return base.reshape(L_DEC, GROUPS, GROUP_W).astype(jnp.bfloat16)


def draw_dec_query(key, part):
    key = jax.random.fold_in(key, 6)
    base = 2.5 * jax.random.truncated_normal(key, -6.0, 6.0, (L_DEC, WIDTH))
    return base.reshape(L_DEC, GROUPS, GROUP_W).astype(jnp.bfloat16)


def draw_dec_keys(key, part):
    key = jax.random.fold_in(key, 7)
    base = jax.random.truncated_normal(key, -6.0, 6.0, (L_DEC, WIDTH))
    return base.reshape(L_DEC, GROUPS, GROUP_W).astype(jnp.bfloat16)


def block_scale(stream_key, shape, cuts, smallest, high):
    level, own = 1.0, jax.random.fold_in(stream_key, 6)
    for position, shards_of in cuts:
        heights = jnp.exp(jax.random.uniform(jax.random.fold_in(own, position), (shards_of,), jnp.float32, smallest / len(cuts), high / len(cuts)))
        level = level * jnp.repeat(heights, shape[position] // shards_of).reshape([-1 if axis == position else 1 for axis in range(len(shape))])
    return level


def noise(rng, extent, spread, bound, cuts=(), held_as=jnp.bfloat16):
    values = spread * jax.random.normal(rng, extent, jnp.float32)
    if cuts:
        values = values * block_scale(rng, extent, cuts, -0.22, 0.18)
    return jnp.clip(values, -bound, bound).astype(held_as)


def setup_inputs(seed: int = 0) -> dict:
    arg_keys = jax.random.split(jax.random.key(seed), 13)
    return {
        "enc_query": draw_enc_query(jax.random.fold_in(arg_keys[12], 71), 0),
        "enc_keys": draw_enc_keys(jax.random.fold_in(arg_keys[12], 71), 0),
        "enc_values": noise(arg_keys[2], (BATCHES, L_ENC, WIDTH), 1.0, 6.0, ((0, 4), (1, 2), (2, 4))),
        "enc_lengths": draw_enc_lengths(jax.random.fold_in(arg_keys[12], 71), 0),
        "cross_keys": draw_cross_keys(jax.random.fold_in(arg_keys[12], 71), 0),
        "cross_values": noise(arg_keys[5], (BATCHES, L_ENC, WIDTH), 1.0, 6.0, ((0, 4), (1, 2), (2, 4))),
        "cross_query": draw_cross_query(jax.random.fold_in(arg_keys[12], 71), 0),
        "dec_query": draw_dec_query(jax.random.fold_in(arg_keys[12], 71), 0),
        "dec_keys": draw_dec_keys(jax.random.fold_in(arg_keys[12], 71), 0),
        "dec_values": noise(arg_keys[9], (L_DEC, GROUPS, GROUP_W), 1.0, 6.0, ((0, 2), (1, 4), (2, 4))),
        "cross_out_weight": noise(arg_keys[10], (GROUPS, GROUP_W, D), WIDTH ** -0.5, 0.125, ((0, 4), (1, 4))),
        "dec_hidden": noise(arg_keys[11], (L_DEC, D), 1.0, 6.0, ((0, 2), (1, 16))),
    }


def attend(queries, key_rows, values, allowed):
    query_len = queries.shape[0]
    key_len = key_rows.shape[0]
    head_count = queries.shape[1] // HEAD_DIM
    query_heads = queries.reshape(query_len, head_count, HEAD_DIM).transpose(1, 0, 2)
    key_heads = key_rows.reshape(key_len, head_count, HEAD_DIM).transpose(1, 0, 2)
    value_heads = values.reshape(key_len, head_count, HEAD_DIM).transpose(1, 0, 2)
    scale = HEAD_DIM ** -0.5

    def single(operands):
        one_query, one_key, one_value = operands
        scores = jnp.dot(one_query, one_key.T, preferred_element_type=jnp.float32) * scale
        scores = jnp.where(allowed, scores, -1e30)
        highest = jnp.max(scores, axis=1, keepdims=True)
        weights = jnp.where(allowed, jnp.exp(scores - highest), 0.0)
        rounded = weights.astype(jnp.bfloat16)
        summed = jnp.dot(rounded, one_value, preferred_element_type=jnp.float32)
        return (summed / jnp.sum(weights, axis=1, keepdims=True)).astype(jnp.bfloat16)

    context = lax.map(single, (query_heads, key_heads, value_heads))
    return context.transpose(1, 0, 2).reshape(query_len, head_count * HEAD_DIM)


def reference(enc_query, enc_keys, enc_values, enc_lengths, cross_keys, cross_values, cross_query, dec_query, dec_keys, dec_values, cross_out_weight, dec_hidden):
    positions = jnp.arange(L_ENC, dtype=jnp.int32)
    enc_parts = []
    for micro in range(BATCHES):
        allowed = (positions < enc_lengths[micro])[None, :]
        enc_parts.append(attend(enc_query[micro], enc_keys[micro], enc_values[micro], allowed))
    enc_context = jnp.stack(enc_parts)
    cross_allowed = (positions < enc_lengths[0])[None, :]
    cross_context = attend(cross_query.reshape(L_DEC, WIDTH), cross_keys[0], cross_values[0], cross_allowed)
    dec_positions = jnp.arange(L_DEC, dtype=jnp.int32)
    causal = dec_positions[None, :] <= dec_positions[:, None]
    self_flat = attend(dec_query.reshape(L_DEC, WIDTH), dec_keys.reshape(L_DEC, WIDTH), dec_values.reshape(L_DEC, WIDTH), causal)
    self_context = self_flat.reshape(L_DEC, GROUPS, GROUP_W)
    projected = jnp.dot(cross_context, cross_out_weight.reshape(WIDTH, D), preferred_element_type=jnp.float32)
    decoded = (dec_hidden.astype(jnp.float32) + projected).astype(jnp.bfloat16)
    return (enc_context, self_context, decoded)
```

```python
import functools
import math

import jax
import jax.numpy as jnp
from jax import lax
from jax.experimental import pallas as pl
from jax.experimental.pallas import tpu as pltpu
from jax.sharding import PartitionSpec as P

HEAD_DIM = 64
PAIR = 2 * HEAD_DIM
FACTOR = HEAD_DIM ** (-0.5) * math.log2(math.e)
LOW = -1e30
SECTIONS = 4
F32 = jnp.float32
BF16 = jnp.bfloat16


def each(low, high, body):
    if high - low <= 4:
        for step in range(low, high):
            body(step)
    else:
        lax.fori_loop(low, high, lambda step, carry: (body(step), carry)[1], 0)


def stack_heads(queries):
    lane = lax.broadcasted_iota(jnp.int32, queries.shape, 1)
    wide = queries.astype(F32)
    first = jnp.where(lane < HEAD_DIM, wide, 0.0).astype(BF16)
    second = jnp.where(lane < HEAD_DIM, 0.0, wide).astype(BF16)
    return jnp.concatenate([first, second], axis=0)


def attend(stacked, keys, values, bias):
    scores = lax.dot_general(stacked, keys, (((1,), (1,)), ((), ())), preferred_element_type=F32)
    scores = scores * FACTOR + bias
    high = jnp.max(scores, axis=1, keepdims=True)
    weights = jnp.exp2(scores - high).astype(BF16)
    wide = jnp.concatenate([values, jnp.ones_like(values)], axis=1)
    return jnp.dot(weights, wide, preferred_element_type=F32), high


def merge_heads(summed):
    context = summed[:, :PAIR] / summed[:, PAIR:]
    rows = context.shape[0] // 2
    lane = lax.broadcasted_iota(jnp.int32, (rows, PAIR), 1)
    return jnp.where(lane < HEAD_DIM, context[:rows], context[rows:]).astype(BF16)


def kernel(
    n, mps,
    eq, ek, ev, lengths, ck, cv, cq, dq, dk, dv, weight, hidden,
    enc_out, self_out, dec_out,
    q_v, ekb, evb, xkb, xvb, cq_v, dq_v, dkb, dvb, w_v, hid_v,
    acc, highs, ctx, ctx_in, y_out, y_in, own, z_out, z_in,
    load_sem, enc_send, enc_recv, x_send, x_recv, dec_send, dec_recv,
    w_send, w_recv, w_load, ctx_send, ctx_recv, y_send, y_recv, z_send, z_recv,
):
    seq, sect, mp = lax.axis_index("seq"), lax.axis_index("sect"), lax.axis_index("mp")
    enc_rows, enc_width = q_v.shape
    dec_rows = cq_v.shape[0]
    block = hid_v.shape[1]
    span = mps * block
    near = sect + 1 - 2 * lax.rem(sect, 2)
    far = lax.rem(sect + 2, SECTIONS)
    core = lax.rem(sect, 2)
    level = sect // 2
    MESH = pl.DeviceIdType.MESH

    def remote(source, target, send, recv, device):
        return pltpu.make_async_remote_copy(
            src_ref=source, dst_ref=target, send_sem=send, recv_sem=recv,
            device_id=device, device_id_type=MESH,
        )

    def peer(step):
        return lax.rem(seq + step, n)

    def landed(ref, sem):
        pltpu.make_async_copy(ref, ref, sem).wait()

    loads = [
        pltpu.make_async_copy(eq, q_v, load_sem.at[0]),
        pltpu.make_async_copy(cq, cq_v, load_sem.at[1]),
        pltpu.make_async_copy(dq, dq_v, load_sem.at[2]),
        pltpu.make_async_copy(hidden, hid_v, load_sem.at[3]),
        pltpu.make_async_copy(ek, ekb.at[seq], enc_recv.at[0, seq]),
        pltpu.make_async_copy(ev, evb.at[seq], enc_recv.at[1, seq]),
        pltpu.make_async_copy(dk, dkb.at[seq], dec_recv.at[0, seq]),
        pltpu.make_async_copy(dv, dvb.at[seq], dec_recv.at[1, seq]),
    ]
    for load in loads:
        load.start()

    def columns(half, side):
        return pl.ds(pl.multiple_of((2 * half + side) * span, span), span)

    depth = weight.shape[0]
    w_loads = [
        pltpu.make_async_copy(
            weight.at[:, columns(half, core)], w_v.at[half, pl.ds(0, depth)], w_load.at[half]
        )
        for half in range(2)
    ]
    for load in w_loads:
        load.start()

    def first_columns(source):
        return source.at[:, pl.ds(0, PAIR)]

    @pl.when(sect == 0)
    def _():
        pltpu.make_async_copy(first_columns(ck), xkb.at[seq], x_recv.at[0, seq]).start()
        pltpu.make_async_copy(first_columns(cv), xvb.at[seq], x_recv.at[1, seq]).start()

    barrier = pltpu.get_barrier_semaphore()

    def greet(seq_step, sect_step):
        pl.semaphore_signal(
            barrier, inc=1,
            device_id={"seq": peer(seq_step), "sect": lax.rem(sect + sect_step, SECTIONS)},
            device_id_type=MESH,
        )

    for sect_step in range(SECTIONS):
        each(1 if sect_step == 0 else 0, n, lambda step: greet(step, sect_step))
    for step in range(1, mps):
        pl.semaphore_signal(
            barrier, inc=1, device_id={"mp": lax.rem(mp + step, mps)}, device_id_type=MESH
        )
    pl.semaphore_wait(barrier, n * SECTIONS - 1 + mps - 1)

    def cross_copies(step, section):
        device = {"seq": peer(step), "sect": section}
        lanes = pl.ds(section * PAIR, PAIR)
        return [
            remote(source.at[:, lanes], target.at[seq], x_send.at[which, section, step],
                   x_recv.at[which, seq], device)
            for which, source, target in ((0, ck, xkb), (1, cv, xvb))
        ]

    def start_cross(step, section):
        for copy in cross_copies(step, section):
            copy.start()

    def end_cross(step, section):
        for copy in cross_copies(step, section):
            copy.wait_send()

    def all_cross(action):
        for section in (2, 3, 1, 0):
            each(1 if section == 0 else 0, n, lambda step: action(step, section))

    @pl.when(sect == 0)
    def _():
        all_cross(start_cross)

    def seq_copies(step):
        device = {"seq": peer(step)}
        dec = [
            remote(source, target.at[seq], dec_send.at[which, step], dec_recv.at[which, seq], device)
            for which, source, target in ((0, dk, dkb), (1, dv, dvb))
        ]
        enc = [
            remote(source, target.at[seq], enc_send.at[which, step], enc_recv.at[which, seq], device)
            for which, source, target in ((0, ek, ekb), (1, ev, evb))
        ]
        return dec + enc

    def start_seq(step):
        for copy in seq_copies(step):
            copy.start()

    def end_seq(step):
        for copy in seq_copies(step):
            copy.wait_send()

    each(1, n, start_seq)
    w_copies = [
        remote(weight.at[:, columns(half, 1 - core)], w_v.at[half, pl.ds(depth, depth)],
               w_send.at[half], w_recv.at[half], {"sect": near})
        for half in range(2)
    ]
    for copy in w_copies:
        copy.start()

    enc_limit = lengths[sect]
    pairs = enc_width // PAIR

    def enc_chunk(source, first):
        landed(ekb.at[source], enc_recv.at[0, source])
        landed(evb.at[source], enc_recv.at[1, source])
        position = source * enc_rows + lax.broadcasted_iota(jnp.int32, (1, enc_rows), 1)
        bias = jnp.where(position < enc_limit, 0.0, LOW)
        for pair in range(pairs):
            lanes = pl.ds(pair * PAIR, PAIR)
            summed, high = attend(
                stack_heads(q_v[:, lanes]), ekb[source, :, lanes], evb[source, :, lanes], bias
            )
            if first:
                acc[pair] = summed
                highs[pair] = jnp.broadcast_to(high, highs.shape[1:])
            else:
                before = highs[pair][:, :1]
                top = jnp.maximum(before, high)
                acc[pair] = acc[pair] * jnp.exp2(before - top) + summed * jnp.exp2(high - top)
                highs[pair] = jnp.broadcast_to(top, highs.shape[1:])

    loads[0].wait()
    enc_chunk(seq, True)

    loads[1].wait()

    def cross_landed(source):
        landed(xkb.at[source], x_recv.at[0, source])
        landed(xvb.at[source], x_recv.at[1, source])

    each(0, n, cross_landed)
    length = n * enc_rows
    position = lax.broadcasted_iota(jnp.int32, (1, length), 1)
    bias = jnp.where(position < lengths[0], 0.0, LOW)
    summed, _ = attend(
        stack_heads(cq_v[...]), xkb[...].reshape(length, PAIR), xvb[...].reshape(length, PAIR), bias
    )
    ctx[...] = merge_heads(summed)
    ctx_copy = remote(ctx, ctx_in, ctx_send, ctx_recv, {"sect": near})
    ctx_copy.start()

    loads[2].wait()

    def dec_landed(source):
        landed(dkb.at[source], dec_recv.at[0, source])
        landed(dvb.at[source], dec_recv.at[1, source])

    each(0, n, dec_landed)
    length = n * dec_rows
    row = lax.broadcasted_iota(jnp.int32, (2 * dec_rows, length), 0)
    row = jnp.where(row >= dec_rows, row - dec_rows, row) + seq * dec_rows
    position = lax.broadcasted_iota(jnp.int32, (2 * dec_rows, length), 1)
    bias = jnp.where(position <= row, 0.0, LOW)
    summed, _ = attend(
        stack_heads(dq_v[...]), dkb[...].reshape(length, PAIR), dvb[...].reshape(length, PAIR), bias
    )
    self_out[...] = merge_heads(summed)

    for load in w_loads:
        load.wait()
    for copy in w_copies:
        copy.wait_recv()
    ctx_copy.wait_recv()
    both = jnp.concatenate([ctx[...], ctx_in[...]], axis=1)
    order = list(range(1, mps)) + [0]

    def project(half, step):
        owner = lax.rem(mp + step, mps)
        lanes = pl.ds(pl.multiple_of(owner * block, block), block)
        return jnp.dot(both, w_v[half, :, lanes], preferred_element_type=F32)

    y_copies = {}
    for step in order:
        y_out[step] = project(1 - level, step).astype(BF16)
        y_copies[step] = remote(
            y_out.at[step], y_in.at[step], y_send.at[step], y_recv.at[step], {"sect": far}
        )
        y_copies[step].start()
    for step in order:
        own[step] = project(level, step)

    each(1, n, lambda step: enc_chunk(peer(step), False))
    for pair in range(pairs):
        enc_out[:, pair * PAIR:(pair + 1) * PAIR] = merge_heads(acc[pair])

    z_copies = {}
    for step in range(1, mps):
        y_copies[step].wait_recv()
        z_out[step] = (own[step] + y_in[step].astype(F32)).astype(BF16)
        z_copies[step] = remote(
            z_out.at[step], z_in.at[step], z_send.at[step], z_recv.at[step],
            {"mp": lax.rem(mp + step, mps)},
        )
        z_copies[step].start()
    loads[3].wait()
    y_copies[0].wait_recv()
    total = own[0] + y_in[0].astype(F32)
    for step in range(1, mps):
        z_copies[step].wait_recv()
        total = total + z_in[step].astype(F32)
    dec_out[...] = (hid_v[...].astype(F32) + total).astype(BF16)

    @pl.when(sect == 0)
    def _():
        all_cross(end_cross)

    each(1, n, end_seq)
    for copy in w_copies + [ctx_copy] + list(y_copies.values()) + list(z_copies.values()):
        copy.wait_send()


def per_device(
    n, mps, enc_query, enc_keys, enc_values, enc_lengths, cross_keys, cross_values,
    cross_query, dec_query, dec_keys, dec_values, cross_out_weight, dec_hidden,
):
    enc_rows, enc_width = enc_query.shape[1:]
    dec_rows, _, narrow = cross_query.shape
    depth, model = cross_out_weight.shape[1:]
    block = dec_hidden.shape[1]
    span = model // SECTIONS
    pairs = enc_width // PAIR
    vmem, dma = pltpu.VMEM, pltpu.SemaphoreType.DMA
    any_space = pl.BlockSpec(memory_space=pl.ANY)
    in_vmem = pl.BlockSpec(memory_space=pltpu.VMEM)
    enc_out, self_out, decoded = pl.pallas_call(
        functools.partial(kernel, n, mps),
        out_shape=(
            jax.ShapeDtypeStruct((enc_rows, enc_width), BF16),
            jax.ShapeDtypeStruct((dec_rows, narrow), BF16),
            jax.ShapeDtypeStruct((dec_rows, block), BF16),
        ),
        in_specs=[any_space] * 3
        + [pl.BlockSpec(memory_space=pltpu.SMEM)]
        + [any_space] * 8,
        out_specs=(in_vmem,) * 3,
        scratch_shapes=[
            vmem((enc_rows, enc_width), BF16),
            vmem((n, enc_rows, enc_width), BF16),
            vmem((n, enc_rows, enc_width), BF16),
            vmem((n, enc_rows, narrow), BF16),
            vmem((n, enc_rows, narrow), BF16),
            vmem((dec_rows, narrow), BF16),
            vmem((dec_rows, narrow), BF16),
            vmem((n, dec_rows, narrow), BF16),
            vmem((n, dec_rows, narrow), BF16),
            vmem((2, 2 * depth, span), BF16),
            vmem((dec_rows, block), BF16),
            vmem((pairs, 2 * enc_rows, 2 * PAIR), F32),
            vmem((pairs, 2 * enc_rows, PAIR), F32),
            vmem((dec_rows, narrow), BF16),
            vmem((dec_rows, narrow), BF16),
            vmem((mps, dec_rows, block), BF16),
            vmem((mps, dec_rows, block), BF16),
            vmem((mps, dec_rows, block), F32),
            vmem((mps, dec_rows, block), BF16),
            vmem((mps, dec_rows, block), BF16),
            dma((4,)),
            dma((2, n)), dma((2, n)),
            dma((2, SECTIONS, n)), dma((2, n)),
            dma((2, n)), dma((2, n)),
            dma((2,)), dma((2,)), dma((2,)),
            dma, dma,
            dma((mps,)), dma((mps,)), dma((mps,)), dma((mps,)),
        ],
        compiler_params=pltpu.CompilerParams(
            collective_id=0, has_side_effects=True,
            vmem_limit_bytes=60 << 20,
        ),
    )(
        enc_query[0], enc_keys[0], enc_values[0], enc_lengths, cross_keys[0], cross_values[0],
        cross_query[:, 0, :], dec_query[:, 0, :], dec_keys[:, 0, :], dec_values[:, 0, :],
        cross_out_weight[0], dec_hidden,
    )
    return enc_out[None], self_out[:, None, :], decoded


def solution(mesh):
    in_specs = (
        P("sect", "seq", "mp"),
        P("sect", "seq", "mp"),
        P("sect", "seq", "mp"),
        P(),
        P("sect", "seq", "mp"),
        P("sect", "seq", "mp"),
        P("seq", "mp", "sect"),
        P("seq", "mp", "sect"),
        P("seq", "mp", "sect"),
        P("seq", "mp", "sect"),
        P("mp", "sect", None),
        P("seq", ("sect", "mp")),
    )
    out_specs = (P("sect", "seq", "mp"), P("seq", "mp", "sect"), P("seq", ("sect", "mp")))
    return jax.shard_map(
        functools.partial(per_device, mesh.shape["seq"], mesh.shape["mp"]),
        mesh=mesh, in_specs=in_specs, out_specs=out_specs, check_vma=False,
    )
```

```python
import functools
import math

import jax
import jax.numpy as jnp
from jax import lax
from jax.experimental import pallas as pl
from jax.experimental.pallas import tpu as pltpu
from jax.sharding import PartitionSpec as P

HEAD_DIM = 64
PAIR = 2 * HEAD_DIM
FACTOR = HEAD_DIM ** (-0.5) * math.log2(math.e)
LOW = -1e30
SECTIONS = 4
F32 = jnp.float32
BF16 = jnp.bfloat16


def each(low, high, body):
    if high - low <= 4:
        for step in range(low, high):
            body(step)
    else:
        lax.fori_loop(low, high, lambda step, carry: (body(step), carry)[1], 0)


def stack_heads(queries):
    lane = lax.broadcasted_iota(jnp.int32, queries.shape, 1)
    wide = queries.astype(F32)
    first = jnp.where(lane < HEAD_DIM, wide, 0.0).astype(BF16)
    second = jnp.where(lane < HEAD_DIM, 0.0, wide).astype(BF16)
    return jnp.concatenate([first, second], axis=0)


def attend(stacked, keys, values, bias):
    scores = lax.dot_general(stacked, keys, (((1,), (1,)), ((), ())), preferred_element_type=F32)
    scores = scores * FACTOR + bias
    high = jnp.max(scores, axis=1, keepdims=True)
    weights = jnp.exp2(scores - high).astype(BF16)
    wide = jnp.concatenate([values, jnp.ones_like(values)], axis=1)
    return jnp.dot(weights, wide, preferred_element_type=F32), high


def merge_heads(summed):
    context = summed[:, :PAIR] / summed[:, PAIR:]
    rows = context.shape[0] // 2
    lane = lax.broadcasted_iota(jnp.int32, (rows, PAIR), 1)
    return jnp.where(lane < HEAD_DIM, context[:rows], context[rows:]).astype(BF16)


def kernel(
    n, mps,
    eq, ek, ev, lengths, ck, cv, cq, dq, dk, dv, weight, hidden,
    enc_out, self_out, dec_out,
    q_v, ekb, evb, xkb, xvb, cq_v, dq_v, dkb, dvb, w_v, hid_v,
    acc, highs, ctx, ctx_in, y_out, y_in, own, z_out, z_in,
    load_sem, enc_send, enc_recv, x_send, x_recv, dec_send, dec_recv,
    w_send, w_recv, w_load, ctx_send, ctx_recv, y_send, y_recv, z_send, z_recv,
):
    seq, sect, mp = lax.axis_index("seq"), lax.axis_index("sect"), lax.axis_index("mp")
    enc_rows, enc_width = q_v.shape
    dec_rows = cq_v.shape[0]
    block = hid_v.shape[1]
    span = mps * block
    near = sect + 1 - 2 * lax.rem(sect, 2)
    far = lax.rem(sect + 2, SECTIONS)
    core = lax.rem(sect, 2)
    level = sect // 2
    MESH = pl.DeviceIdType.MESH

    def remote(source, target, send, recv, device):
        return pltpu.make_async_remote_copy(
            src_ref=source, dst_ref=target, send_sem=send, recv_sem=recv,
            device_id=device, device_id_type=MESH,
        )

    def peer(step):
        return lax.rem(seq + step, n)

    def landed(ref, sem):
        pltpu.make_async_copy(ref, ref, sem).wait()

    loads = [
        pltpu.make_async_copy(eq, q_v, load_sem.at[0]),
        pltpu.make_async_copy(cq, cq_v, load_sem.at[1]),
        pltpu.make_async_copy(dq, dq_v, load_sem.at[2]),
        pltpu.make_async_copy(hidden, hid_v, load_sem.at[3]),
        pltpu.make_async_copy(ek, ekb.at[seq], enc_recv.at[0, seq]),
        pltpu.make_async_copy(ev, evb.at[seq], enc_recv.at[1, seq]),
        pltpu.make_async_copy(dk, dkb.at[seq], dec_recv.at[0, seq]),
        pltpu.make_async_copy(dv, dvb.at[seq], dec_recv.at[1, seq]),
    ]
    for load in loads:
        load.start()

    def columns(half, side):
        return pl.ds(pl.multiple_of((2 * half + side) * span, span), span)

    depth = weight.shape[0]
    w_loads = [
        pltpu.make_async_copy(
            weight.at[:, columns(half, core)], w_v.at[half, pl.ds(0, depth)], w_load.at[half]
        )
        for half in range(2)
    ]
    for load in w_loads:
        load.start()

    def first_columns(source):
        return source.at[:, pl.ds(0, PAIR)]

    @pl.when(sect == 0)
    def _():
        pltpu.make_async_copy(first_columns(ck), xkb.at[seq], x_recv.at[0, seq]).start()
        pltpu.make_async_copy(first_columns(cv), xvb.at[seq], x_recv.at[1, seq]).start()

    barrier = pltpu.get_barrier_semaphore()

    def greet(seq_step, sect_step):
        pl.semaphore_signal(
            barrier, inc=1,
            device_id={"seq": peer(seq_step), "sect": lax.rem(sect + sect_step, SECTIONS)},
            device_id_type=MESH,
        )

    for sect_step in range(SECTIONS):
        each(1 if sect_step == 0 else 0, n, lambda step: greet(step, sect_step))
    for step in range(1, mps):
        pl.semaphore_signal(
            barrier, inc=1, device_id={"mp": lax.rem(mp + step, mps)}, device_id_type=MESH
        )
    pl.semaphore_wait(barrier, n * SECTIONS - 1 + mps - 1)

    def cross_copies(step, section):
        device = {"seq": peer(step), "sect": section}
        lanes = pl.ds(section * PAIR, PAIR)
        return [
            remote(source.at[:, lanes], target.at[seq], x_send.at[which, section, step],
                   x_recv.at[which, seq], device)
            for which, source, target in ((0, ck, xkb), (1, cv, xvb))
        ]

    def start_cross(step, section):
        for copy in cross_copies(step, section):
            copy.start()

    def end_cross(step, section):
        for copy in cross_copies(step, section):
            copy.wait_send()

    def all_cross(action):
        for section in (2, 3, 1, 0):
            each(1 if section == 0 else 0, n, lambda step: action(step, section))

    @pl.when(sect == 0)
    def _():
        all_cross(start_cross)

    def seq_copies(group, step):
        device = {"seq": peer(step)}
        if group == 0:
            return [
                remote(source, target.at[seq], dec_send.at[which, step], dec_recv.at[which, seq], device)
                for which, source, target in ((0, dk, dkb), (1, dv, dvb))
            ]
        return [
            remote(source, target.at[seq], enc_send.at[which, step], enc_recv.at[which, seq], device)
            for which, source, target in ((0, ek, ekb), (1, ev, evb))
        ]

    def start_seq(group, step):
        for copy in seq_copies(group, step):
            copy.start()

    def end_seq(step):
        for copy in seq_copies(0, step) + seq_copies(1, step):
            copy.wait_send()

    each(1, n, functools.partial(start_seq, 0))
    w_copies = [
        remote(weight.at[:, columns(half, 1 - core)], w_v.at[half, pl.ds(depth, depth)],
               w_send.at[half], w_recv.at[half], {"sect": near})
        for half in range(2)
    ]
    for copy in w_copies:
        copy.start()

    enc_limit = lengths[sect]
    pairs = enc_width // PAIR

    def enc_chunk(source, first):
        landed(ekb.at[source], enc_recv.at[0, source])
        landed(evb.at[source], enc_recv.at[1, source])
        position = source * enc_rows + lax.broadcasted_iota(jnp.int32, (1, enc_rows), 1)
        bias = jnp.where(position < enc_limit, 0.0, LOW)
        for pair in range(pairs):
            lanes = pl.ds(pair * PAIR, PAIR)
            summed, high = attend(
                stack_heads(q_v[:, lanes]), ekb[source, :, lanes], evb[source, :, lanes], bias
            )
            if first:
                acc[pair] = summed
                highs[pair] = jnp.broadcast_to(high, highs.shape[1:])
            else:
                before = highs[pair][:, :1]
                top = jnp.maximum(before, high)
                acc[pair] = acc[pair] * jnp.exp2(before - top) + summed * jnp.exp2(high - top)
                highs[pair] = jnp.broadcast_to(top, highs.shape[1:])

    loads[0].wait()
    enc_chunk(seq, True)

    loads[1].wait()

    def cross_landed(source):
        landed(xkb.at[source], x_recv.at[0, source])
        landed(xvb.at[source], x_recv.at[1, source])

    each(0, n, cross_landed)
    each(1, n, functools.partial(start_seq, 1))
    length = n * enc_rows
    position = lax.broadcasted_iota(jnp.int32, (1, length), 1)
    bias = jnp.where(position < lengths[0], 0.0, LOW)
    summed, _ = attend(
        stack_heads(cq_v[...]), xkb[...].reshape(length, PAIR), xvb[...].reshape(length, PAIR), bias
    )
    ctx[...] = merge_heads(summed)
    ctx_copy = remote(ctx, ctx_in, ctx_send, ctx_recv, {"sect": near})
    ctx_copy.start()

    loads[2].wait()

    def dec_landed(source):
        landed(dkb.at[source], dec_recv.at[0, source])
        landed(dvb.at[source], dec_recv.at[1, source])

    each(0, n, dec_landed)
    length = n * dec_rows
    row = lax.broadcasted_iota(jnp.int32, (2 * dec_rows, length), 0)
    row = jnp.where(row >= dec_rows, row - dec_rows, row) + seq * dec_rows
    position = lax.broadcasted_iota(jnp.int32, (2 * dec_rows, length), 1)
    bias = jnp.where(position <= row, 0.0, LOW)
    summed, _ = attend(
        stack_heads(dq_v[...]), dkb[...].reshape(length, PAIR), dvb[...].reshape(length, PAIR), bias
    )
    self_out[...] = merge_heads(summed)

    for load in w_loads:
        load.wait()
    for copy in w_copies:
        copy.wait_recv()
    ctx_copy.wait_recv()
    both = jnp.concatenate([ctx[...], ctx_in[...]], axis=1)
    order = list(range(1, mps)) + [0]

    def project(half, step):
        owner = lax.rem(mp + step, mps)
        lanes = pl.ds(pl.multiple_of(owner * block, block), block)
        return jnp.dot(both, w_v[half, :, lanes], preferred_element_type=F32)

    y_copies = {}
    for step in order:
        y_out[step] = project(1 - level, step).astype(BF16)
        y_copies[step] = remote(
            y_out.at[step], y_in.at[step], y_send.at[step], y_recv.at[step], {"sect": far}
        )
        y_copies[step].start()
    for step in order:
        own[step] = project(level, step)

    z_copies = {}
    for step in range(1, mps):
        y_copies[step].wait_recv()
        z_out[step] = (own[step] + y_in[step].astype(F32)).astype(BF16)
        z_copies[step] = remote(
            z_out.at[step], z_in.at[step], z_send.at[step], z_recv.at[step],
            {"mp": lax.rem(mp + step, mps)},
        )
        z_copies[step].start()
    each(1, n, lambda step: enc_chunk(peer(step), False))
    for pair in range(pairs):
        enc_out[:, pair * PAIR:(pair + 1) * PAIR] = merge_heads(acc[pair])

    loads[3].wait()
    y_copies[0].wait_recv()
    total = own[0] + y_in[0].astype(F32)
    for step in range(1, mps):
        z_copies[step].wait_recv()
        total = total + z_in[step].astype(F32)
    dec_out[...] = (hid_v[...].astype(F32) + total).astype(BF16)

    @pl.when(sect == 0)
    def _():
        all_cross(end_cross)

    each(1, n, end_seq)
    for copy in w_copies + [ctx_copy] + list(y_copies.values()) + list(z_copies.values()):
        copy.wait_send()


def store(*refs):
    sources, targets, sems = refs[:3], refs[3:6], refs[6]
    copies = [
        pltpu.make_async_copy(source, target, sems.at[which])
        for which, (source, target) in enumerate(zip(sources, targets))
    ]
    for copy in copies:
        copy.start()
    for copy in copies:
        copy.wait()


def per_device(
    n, mps, enc_query, enc_keys, enc_values, enc_lengths, cross_keys, cross_values,
    cross_query, dec_query, dec_keys, dec_values, cross_out_weight, dec_hidden,
):
    enc_rows, enc_width = enc_query.shape[1:]
    dec_rows, _, narrow = cross_query.shape
    depth, model = cross_out_weight.shape[1:]
    block = dec_hidden.shape[1]
    span = model // SECTIONS
    pairs = enc_width // PAIR
    vmem, dma = pltpu.VMEM, pltpu.SemaphoreType.DMA
    in_hbm = pl.BlockSpec(memory_space=pltpu.HBM)
    in_vmem = pl.BlockSpec(memory_space=pltpu.VMEM)
    shapes = ((enc_rows, enc_width), (dec_rows, narrow), (dec_rows, block))
    results = pl.pallas_call(
        functools.partial(kernel, n, mps),
        out_shape=tuple(vmem(shape, BF16) for shape in shapes),
        in_specs=[in_hbm] * 3
        + [pl.BlockSpec(memory_space=pltpu.SMEM)]
        + [in_hbm] * 8,
        out_specs=(in_vmem,) * 3,
        scratch_shapes=[
            vmem((enc_rows, enc_width), BF16),
            vmem((n, enc_rows, enc_width), BF16),
            vmem((n, enc_rows, enc_width), BF16),
            vmem((n, enc_rows, narrow), BF16),
            vmem((n, enc_rows, narrow), BF16),
            vmem((dec_rows, narrow), BF16),
            vmem((dec_rows, narrow), BF16),
            vmem((n, dec_rows, narrow), BF16),
            vmem((n, dec_rows, narrow), BF16),
            vmem((2, 2 * depth, span), BF16),
            vmem((dec_rows, block), BF16),
            vmem((pairs, 2 * enc_rows, 2 * PAIR), F32),
            vmem((pairs, 2 * enc_rows, PAIR), F32),
            vmem((dec_rows, narrow), BF16),
            vmem((dec_rows, narrow), BF16),
            vmem((mps, dec_rows, block), BF16),
            vmem((mps, dec_rows, block), BF16),
            vmem((mps, dec_rows, block), F32),
            vmem((mps, dec_rows, block), BF16),
            vmem((mps, dec_rows, block), BF16),
            dma((4,)),
            dma((2, n)), dma((2, n)),
            dma((2, SECTIONS, n)), dma((2, n)),
            dma((2, n)), dma((2, n)),
            dma((2,)), dma((2,)), dma((2,)),
            dma, dma,
            dma((mps,)), dma((mps,)), dma((mps,)), dma((mps,)),
        ],
        compiler_params=pltpu.CompilerParams(
            collective_id=0, has_side_effects=True,
            vmem_limit_bytes=60 << 20,
        ),
    )(
        enc_query[0], enc_keys[0], enc_values[0], enc_lengths, cross_keys[0], cross_values[0],
        cross_query[:, 0, :], dec_query[:, 0, :], dec_keys[:, 0, :], dec_values[:, 0, :],
        cross_out_weight[0], dec_hidden,
    )
    enc_out, self_out, decoded = pl.pallas_call(
        store,
        out_shape=tuple(jax.ShapeDtypeStruct(shape, BF16) for shape in shapes),
        in_specs=[in_vmem] * 3,
        out_specs=(in_hbm,) * 3,
        scratch_shapes=[dma((3,))],
    )(*results)
    return enc_out[None], self_out[:, None, :], decoded


def solution(mesh):
    in_specs = (
        P("sect", "seq", "mp"),
        P("sect", "seq", "mp"),
        P("sect", "seq", "mp"),
        P(),
        P("sect", "seq", "mp"),
        P("sect", "seq", "mp"),
        P("seq", "mp", "sect"),
        P("seq", "mp", "sect"),
        P("seq", "mp", "sect"),
        P("seq", "mp", "sect"),
        P("mp", "sect", None),
        P("seq", ("sect", "mp")),
    )
    out_specs = (P("sect", "seq", "mp"), P("seq", "mp", "sect"), P("seq", ("sect", "mp")))
    return jax.shard_map(
        functools.partial(per_device, mesh.shape["seq"], mesh.shape["mp"]),
        mesh=mesh, in_specs=in_specs, out_specs=out_specs, check_vma=False,
    )
```

```python
import functools
import math

import jax
import jax.numpy as jnp
from jax import lax
from jax.experimental import pallas as pl
from jax.experimental.pallas import tpu as pltpu
from jax.sharding import PartitionSpec as P

HEAD_DIM = 64
PAIR = 2 * HEAD_DIM
FACTOR = HEAD_DIM ** (-0.5) * math.log2(math.e)
LOW = -1e30
SECTIONS = 4
F32 = jnp.float32
BF16 = jnp.bfloat16


def each(low, high, body):
    if high - low <= 4:
        for step in range(low, high):
            body(step)
    else:
        lax.fori_loop(low, high, lambda step, carry: (body(step), carry)[1], 0)


def stack_heads(queries):
    lane = lax.broadcasted_iota(jnp.int32, queries.shape, 1)
    wide = queries.astype(F32)
    first = jnp.where(lane < HEAD_DIM, wide, 0.0).astype(BF16)
    second = jnp.where(lane < HEAD_DIM, 0.0, wide).astype(BF16)
    return jnp.concatenate([first, second], axis=0)


def attend(stacked, keys, values, bias):
    scores = lax.dot_general(stacked, keys, (((1,), (1,)), ((), ())), preferred_element_type=F32)
    scores = scores * FACTOR + bias
    high = jnp.max(scores, axis=1, keepdims=True)
    weights = jnp.exp2(scores - high).astype(BF16)
    wide = jnp.concatenate([values, jnp.ones_like(values)], axis=1)
    return jnp.dot(weights, wide, preferred_element_type=F32), high


def merge_heads(summed):
    context = summed[:, :PAIR] / summed[:, PAIR:]
    rows = context.shape[0] // 2
    lane = lax.broadcasted_iota(jnp.int32, (rows, PAIR), 1)
    return jnp.where(lane < HEAD_DIM, context[:rows], context[rows:]).astype(BF16)


def kernel(
    n, mps,
    eq, ek, ev, lengths, ck, cv, cq, dq, dk, dv, weight, hidden,
    enc_out, self_out, dec_out,
    q_v, ekb, evb, xkb, xvb, cq_v, dq_v, dkb, dvb, w_v, hid_v,
    acc, highs, ctx, ctx_in, y_out, y_in, own, z_out, z_in,
    load_sem, enc_send, enc_recv, x_send, x_recv, dec_send, dec_recv,
    w_send, w_recv, w_load, ctx_send, ctx_recv, y_send, y_recv, z_send, z_recv,
):
    seq, sect, mp = lax.axis_index("seq"), lax.axis_index("sect"), lax.axis_index("mp")
    enc_rows, enc_width = q_v.shape
    dec_rows = cq_v.shape[0]
    block = hid_v.shape[1]
    span = mps * block
    near = sect + 1 - 2 * lax.rem(sect, 2)
    far = lax.rem(sect + 2, SECTIONS)
    core = lax.rem(sect, 2)
    level = sect // 2
    MESH = pl.DeviceIdType.MESH

    def remote(source, target, send, recv, device):
        return pltpu.make_async_remote_copy(
            src_ref=source, dst_ref=target, send_sem=send, recv_sem=recv,
            device_id=device, device_id_type=MESH,
        )

    def peer(step):
        return lax.rem(seq + step, n)

    def landed(ref, sem):
        pltpu.make_async_copy(ref, ref, sem).wait()

    loads = [
        pltpu.make_async_copy(eq, q_v, load_sem.at[0]),
        pltpu.make_async_copy(cq, cq_v, load_sem.at[1]),
        pltpu.make_async_copy(dq, dq_v, load_sem.at[2]),
        pltpu.make_async_copy(hidden, hid_v, load_sem.at[3]),
        pltpu.make_async_copy(ek, ekb.at[seq], enc_recv.at[0, seq]),
        pltpu.make_async_copy(ev, evb.at[seq], enc_recv.at[1, seq]),
        pltpu.make_async_copy(dk, dkb.at[seq], dec_recv.at[0, seq]),
        pltpu.make_async_copy(dv, dvb.at[seq], dec_recv.at[1, seq]),
    ]
    for load in loads:
        load.start()

    def columns(half, side):
        return pl.ds(pl.multiple_of((2 * half + side) * span, span), span)

    depth = weight.shape[0]
    w_loads = [
        pltpu.make_async_copy(
            weight.at[:, columns(half, core)], w_v.at[half, pl.ds(0, depth)], w_load.at[half]
        )
        for half in range(2)
    ]
    for load in w_loads:
        load.start()

    def first_columns(source):
        return source.at[:, pl.ds(0, PAIR)]

    @pl.when(sect == 0)
    def _():
        pltpu.make_async_copy(first_columns(ck), xkb.at[seq], x_recv.at[0, seq]).start()
        pltpu.make_async_copy(first_columns(cv), xvb.at[seq], x_recv.at[1, seq]).start()

    barrier = pltpu.get_barrier_semaphore()

    def greet(seq_step, sect_step):
        pl.semaphore_signal(
            barrier, inc=1,
            device_id={"seq": peer(seq_step), "sect": lax.rem(sect + sect_step, SECTIONS)},
            device_id_type=MESH,
        )

    for sect_step in range(SECTIONS):
        each(1 if sect_step == 0 else 0, n, lambda step: greet(step, sect_step))
    for step in range(1, mps):
        pl.semaphore_signal(
            barrier, inc=1, device_id={"mp": lax.rem(mp + step, mps)}, device_id_type=MESH
        )
    pl.semaphore_wait(barrier, n * SECTIONS - 1 + mps - 1)

    def cross_copies(step, section):
        device = {"seq": peer(step), "sect": section}
        lanes = pl.ds(section * PAIR, PAIR)
        return [
            remote(source.at[:, lanes], target.at[seq], x_send.at[which, section, step],
                   x_recv.at[which, seq], device)
            for which, source, target in ((0, ck, xkb), (1, cv, xvb))
        ]

    def start_cross(step, section):
        for copy in cross_copies(step, section):
            copy.start()

    def end_cross(step, section):
        for copy in cross_copies(step, section):
            copy.wait_send()

    def all_cross(action):
        for section in (2, 3, 1, 0):
            each(1 if section == 0 else 0, n, lambda step: action(step, section))

    @pl.when(sect == 0)
    def _():
        all_cross(start_cross)

    def seq_copies(group, step):
        device = {"seq": peer(step)}
        if group == 0:
            return [
                remote(source, target.at[seq], dec_send.at[which, step], dec_recv.at[which, seq], device)
                for which, source, target in ((0, dk, dkb), (1, dv, dvb))
            ]
        return [
            remote(source, target.at[seq], enc_send.at[which, step], enc_recv.at[which, seq], device)
            for which, source, target in ((0, ek, ekb), (1, ev, evb))
        ]

    def start_seq(group, step):
        for copy in seq_copies(group, step):
            copy.start()

    def end_seq(step):
        for copy in seq_copies(0, step) + seq_copies(1, step):
            copy.wait_send()

    each(1, n, functools.partial(start_seq, 0))
    w_copies = [
        remote(weight.at[:, columns(half, 1 - core)], w_v.at[half, pl.ds(depth, depth)],
               w_send.at[half], w_recv.at[half], {"sect": near})
        for half in range(2)
    ]
    for copy in w_copies:
        copy.start()

    enc_limit = lengths[sect]
    pairs = enc_width // PAIR

    def enc_chunk(source, first):
        landed(ekb.at[source], enc_recv.at[0, source])
        landed(evb.at[source], enc_recv.at[1, source])
        position = source * enc_rows + lax.broadcasted_iota(jnp.int32, (1, enc_rows), 1)
        bias = jnp.where(position < enc_limit, 0.0, LOW)
        for pair in range(pairs):
            lanes = pl.ds(pair * PAIR, PAIR)
            summed, high = attend(
                stack_heads(q_v[:, lanes]), ekb[source, :, lanes], evb[source, :, lanes], bias
            )
            if first:
                acc[pair] = summed
                highs[pair] = jnp.broadcast_to(high, highs.shape[1:])
            else:
                before = highs[pair][:, :1]
                top = jnp.maximum(before, high)
                acc[pair] = acc[pair] * jnp.exp2(before - top) + summed * jnp.exp2(high - top)
                highs[pair] = jnp.broadcast_to(top, highs.shape[1:])

    loads[0].wait()
    enc_chunk(seq, True)

    loads[1].wait()

    def cross_landed(source):
        landed(xkb.at[source], x_recv.at[0, source])
        landed(xvb.at[source], x_recv.at[1, source])

    each(0, n, cross_landed)
    each(1, n, functools.partial(start_seq, 1))
    length = n * enc_rows
    position = lax.broadcasted_iota(jnp.int32, (1, length), 1)
    bias = jnp.where(position < lengths[0], 0.0, LOW)
    summed, _ = attend(
        stack_heads(cq_v[...]), xkb[...].reshape(length, PAIR), xvb[...].reshape(length, PAIR), bias
    )
    ctx[...] = merge_heads(summed)
    ctx_copy = remote(ctx, ctx_in, ctx_send, ctx_recv, {"sect": near})
    ctx_copy.start()

    loads[2].wait()

    def dec_landed(source):
        landed(dkb.at[source], dec_recv.at[0, source])
        landed(dvb.at[source], dec_recv.at[1, source])

    each(0, n, dec_landed)
    length = n * dec_rows
    row = lax.broadcasted_iota(jnp.int32, (2 * dec_rows, length), 0)
    row = jnp.where(row >= dec_rows, row - dec_rows, row) + seq * dec_rows
    position = lax.broadcasted_iota(jnp.int32, (2 * dec_rows, length), 1)
    bias = jnp.where(position <= row, 0.0, LOW)
    summed, _ = attend(
        stack_heads(dq_v[...]), dkb[...].reshape(length, PAIR), dvb[...].reshape(length, PAIR), bias
    )
    self_out[...] = merge_heads(summed)

    for load in w_loads:
        load.wait()
    for copy in w_copies:
        copy.wait_recv()
    ctx_copy.wait_recv()
    both = jnp.concatenate([ctx[...], ctx_in[...]], axis=1)
    order = list(range(1, mps)) + [0]

    def project(half, step):
        owner = lax.rem(mp + step, mps)
        lanes = pl.ds(pl.multiple_of(owner * block, block), block)
        return jnp.dot(both, w_v[half, :, lanes], preferred_element_type=F32)

    y_copies = {}
    for step in order:
        y_out[step] = project(1 - level, step).astype(BF16)
        y_copies[step] = remote(
            y_out.at[step], y_in.at[step], y_send.at[step], y_recv.at[step], {"sect": far}
        )
        y_copies[step].start()
    for step in order:
        own[step] = project(level, step)

    z_copies = {}
    for step in range(1, mps):
        y_copies[step].wait_recv()
        z_out[step] = (own[step] + y_in[step].astype(F32)).astype(BF16)
        z_copies[step] = remote(
            z_out.at[step], z_in.at[step], z_send.at[step], z_recv.at[step],
            {"mp": lax.rem(mp + step, mps)},
        )
        z_copies[step].start()
    each(1, n, lambda step: enc_chunk(peer(step), False))
    for pair in range(pairs):
        enc_out[:, pair * PAIR:(pair + 1) * PAIR] = merge_heads(acc[pair])

    loads[3].wait()
    y_copies[0].wait_recv()
    total = own[0] + y_in[0].astype(F32)
    for step in range(1, mps):
        z_copies[step].wait_recv()
        total = total + z_in[step].astype(F32)
    dec_out[...] = (hid_v[...].astype(F32) + total).astype(BF16)

    @pl.when(sect == 0)
    def _():
        all_cross(end_cross)

    each(1, n, end_seq)
    for copy in w_copies + [ctx_copy] + list(y_copies.values()) + list(z_copies.values()):
        copy.wait_send()


def store(*refs):
    sources, targets, sems = refs[:3], refs[3:6], refs[6]
    copies = [
        pltpu.make_async_copy(source, target, sems.at[which])
        for which, (source, target) in enumerate(zip(sources, targets))
    ]
    for copy in copies:
        copy.start()
    for copy in copies:
        copy.wait()


def per_device(
    n, mps, enc_query, enc_keys, enc_values, enc_lengths, cross_keys, cross_values,
    cross_query, dec_query, dec_keys, dec_values, cross_out_weight, dec_hidden,
):
    enc_rows, enc_width = enc_query.shape[1:]
    dec_rows, _, narrow = cross_query.shape
    depth, model = cross_out_weight.shape[1:]
    block = dec_hidden.shape[1]
    span = model // SECTIONS
    pairs = enc_width // PAIR
    vmem, dma = pltpu.VMEM, pltpu.SemaphoreType.DMA
    in_hbm = pl.BlockSpec(memory_space=pltpu.HBM)
    in_vmem = pl.BlockSpec(memory_space=pltpu.VMEM)
    shapes = ((enc_rows, enc_width), (dec_rows, narrow), (dec_rows, block))
    results = pl.pallas_call(
        functools.partial(kernel, n, mps),
        out_shape=tuple(vmem(shape, BF16) for shape in shapes),
        in_specs=[in_hbm] * 3
        + [pl.BlockSpec(memory_space=pltpu.SMEM)]
        + [in_hbm] * 8,
        out_specs=(in_vmem,) * 3,
        scratch_shapes=[
            vmem((enc_rows, enc_width), BF16),
            vmem((n, enc_rows, enc_width), BF16),
            vmem((n, enc_rows, enc_width), BF16),
            vmem((n, enc_rows, narrow), BF16),
            vmem((n, enc_rows, narrow), BF16),
            vmem((dec_rows, narrow), BF16),
            vmem((dec_rows, narrow), BF16),
            vmem((n, dec_rows, narrow), BF16),
            vmem((n, dec_rows, narrow), BF16),
            vmem((2, 2 * depth, span), BF16),
            vmem((dec_rows, block), BF16),
            vmem((pairs, 2 * enc_rows, 2 * PAIR), F32),
            vmem((pairs, 2 * enc_rows, PAIR), F32),
            vmem((dec_rows, narrow), BF16),
            vmem((dec_rows, narrow), BF16),
            vmem((mps, dec_rows, block), BF16),
            vmem((mps, dec_rows, block), BF16),
            vmem((mps, dec_rows, block), F32),
            vmem((mps, dec_rows, block), BF16),
            vmem((mps, dec_rows, block), BF16),
            dma((4,)),
            dma((2, n)), dma((2, n)),
            dma((2, SECTIONS, n)), dma((2, n)),
            dma((2, n)), dma((2, n)),
            dma((2,)), dma((2,)), dma((2,)),
            dma, dma,
            dma((mps,)), dma((mps,)), dma((mps,)), dma((mps,)),
        ],
        compiler_params=pltpu.CompilerParams(
            collective_id=0, has_side_effects=True,
            vmem_limit_bytes=60 << 20,
        ),
    )(
        enc_query[0], enc_keys[0], enc_values[0], enc_lengths, cross_keys[0], cross_values[0],
        cross_query[:, 0, :], dec_query[:, 0, :], dec_keys[:, 0, :], dec_values[:, 0, :],
        cross_out_weight[0], dec_hidden,
    )
    enc_out, self_out, decoded = pl.pallas_call(
        store,
        out_shape=tuple(jax.ShapeDtypeStruct(shape, BF16) for shape in shapes),
        in_specs=[in_vmem] * 3,
        out_specs=(in_hbm,) * 3,
        scratch_shapes=[dma((3,))],
        compiler_params=pltpu.CompilerParams(vmem_limit_bytes=1 << 20),
    )(*results)
    return enc_out[None], self_out[:, None, :], decoded


def solution(mesh):
    in_specs = (
        P("sect", "seq", "mp"),
        P("sect", "seq", "mp"),
        P("sect", "seq", "mp"),
        P(),
        P("sect", "seq", "mp"),
        P("sect", "seq", "mp"),
        P("seq", "mp", "sect"),
        P("seq", "mp", "sect"),
        P("seq", "mp", "sect"),
        P("seq", "mp", "sect"),
        P("mp", "sect", None),
        P("seq", ("sect", "mp")),
    )
    out_specs = (P("sect", "seq", "mp"), P("seq", "mp", "sect"), P("seq", ("sect", "mp")))
    return jax.shard_map(
        functools.partial(per_device, mesh.shape["seq"], mesh.shape["mp"]),
        mesh=mesh, in_specs=in_specs, out_specs=out_specs, check_vma=False,
    )
```

```python
import functools
import math

import jax
import jax.numpy as jnp
from jax import lax
from jax.experimental import pallas as pl
from jax.experimental.pallas import tpu as pltpu
from jax.sharding import PartitionSpec as P

HEAD_DIM = 64
PAIR = 2 * HEAD_DIM
FACTOR = HEAD_DIM ** (-0.5) * math.log2(math.e)
LOW = -1e30
SECTIONS = 4
F32 = jnp.float32
BF16 = jnp.bfloat16


def each(low, high, body):
    if high - low <= 4:
        for step in range(low, high):
            body(step)
    else:
        lax.fori_loop(low, high, lambda step, carry: (body(step), carry)[1], 0)


def stack_heads(queries):
    lane = lax.broadcasted_iota(jnp.int32, queries.shape, 1)
    wide = queries.astype(F32)
    first = jnp.where(lane < HEAD_DIM, wide, 0.0).astype(BF16)
    second = jnp.where(lane < HEAD_DIM, 0.0, wide).astype(BF16)
    return jnp.concatenate([first, second], axis=0)


def attend(stacked, keys, values, bias):
    scores = lax.dot_general(stacked, keys, (((1,), (1,)), ((), ())), preferred_element_type=F32)
    scores = scores * FACTOR + bias
    high = jnp.max(scores, axis=1, keepdims=True)
    weights = jnp.exp2(scores - high).astype(BF16)
    wide = jnp.concatenate([values, jnp.ones_like(values)], axis=1)
    return jnp.dot(weights, wide, preferred_element_type=F32), high


def merge_heads(summed):
    context = summed[:, :PAIR] / summed[:, PAIR:]
    rows = context.shape[0] // 2
    lane = lax.broadcasted_iota(jnp.int32, (rows, PAIR), 1)
    return jnp.where(lane < HEAD_DIM, context[:rows], context[rows:]).astype(BF16)


def kernel(
    n, mps,
    eq, ek, ev, lengths, ck, cv, cq, dq, dk, dv, weight, hidden,
    enc_out, self_out, dec_out,
    q_v, ekb, evb, xkb, xvb, cq_v, dq_v, dkb, dvb, w_v, hid_v,
    acc, highs, ctx, ctx_in, y_out, y_in, own, z_out, z_in,
    load_sem, enc_send, enc_recv, x_send, x_recv, dec_send, dec_recv,
    w_send, w_recv, w_load, ctx_send, ctx_recv, y_send, y_recv, z_send, z_recv,
):
    seq, sect, mp = lax.axis_index("seq"), lax.axis_index("sect"), lax.axis_index("mp")
    enc_rows, enc_width = q_v.shape
    dec_rows = cq_v.shape[0]
    block = hid_v.shape[1]
    span = mps * block
    near = sect + 1 - 2 * lax.rem(sect, 2)
    far = lax.rem(sect + 2, SECTIONS)
    core = lax.rem(sect, 2)
    level = sect // 2
    MESH = pl.DeviceIdType.MESH

    def remote(source, target, send, recv, device):
        return pltpu.make_async_remote_copy(
            src_ref=source, dst_ref=target, send_sem=send, recv_sem=recv,
            device_id=device, device_id_type=MESH,
        )

    def peer(step):
        return lax.rem(seq + step, n)

    def landed(ref, sem):
        pltpu.make_async_copy(ref, ref, sem).wait()

    loads = [
        pltpu.make_async_copy(eq, q_v, load_sem.at[0]),
        pltpu.make_async_copy(cq, cq_v, load_sem.at[1]),
        pltpu.make_async_copy(dq, dq_v, load_sem.at[2]),
        pltpu.make_async_copy(hidden, hid_v, load_sem.at[3]),
        pltpu.make_async_copy(ek, ekb.at[seq], enc_recv.at[0, seq]),
        pltpu.make_async_copy(ev, evb.at[seq], enc_recv.at[1, seq]),
        pltpu.make_async_copy(dk, dkb.at[seq], dec_recv.at[0, seq]),
        pltpu.make_async_copy(dv, dvb.at[seq], dec_recv.at[1, seq]),
    ]
    for load in loads:
        load.start()

    def columns(half, side):
        return pl.ds(pl.multiple_of((2 * half + side) * span, span), span)

    depth = weight.shape[0]
    w_loads = [
        pltpu.make_async_copy(
            weight.at[:, columns(half, core)], w_v.at[half, pl.ds(0, depth)], w_load.at[half]
        )
        for half in range(2)
    ]
    for load in w_loads:
        load.start()

    def first_columns(source):
        return source.at[:, pl.ds(0, PAIR)]

    @pl.when(sect == 0)
    def _():
        pltpu.make_async_copy(first_columns(ck), xkb.at[seq], x_recv.at[0, seq]).start()
        pltpu.make_async_copy(first_columns(cv), xvb.at[seq], x_recv.at[1, seq]).start()

    barrier = pltpu.get_barrier_semaphore()

    def greet(seq_step, sect_step):
        pl.semaphore_signal(
            barrier, inc=1,
            device_id={"seq": peer(seq_step), "sect": lax.rem(sect + sect_step, SECTIONS)},
            device_id_type=MESH,
        )

    for sect_step in range(SECTIONS):
        each(1 if sect_step == 0 else 0, n, lambda step: greet(step, sect_step))
    for step in range(1, mps):
        pl.semaphore_signal(
            barrier, inc=1, device_id={"mp": lax.rem(mp + step, mps)}, device_id_type=MESH
        )
    pl.semaphore_wait(barrier, n * SECTIONS - 1 + mps - 1)

    def cross_copies(step, section):
        device = {"seq": peer(step), "sect": section}
        lanes = pl.ds(section * PAIR, PAIR)
        return [
            remote(source.at[:, lanes], target.at[seq], x_send.at[which, section, step],
                   x_recv.at[which, seq], device)
            for which, source, target in ((0, ck, xkb), (1, cv, xvb))
        ]

    def start_cross(step, section):
        for copy in cross_copies(step, section):
            copy.start()

    def end_cross(step, section):
        for copy in cross_copies(step, section):
            copy.wait_send()

    def all_cross(action):
        for section in (2, 3, 1, 0):
            each(1 if section == 0 else 0, n, lambda step: action(step, section))

    @pl.when(sect == 0)
    def _():
        all_cross(start_cross)

    def seq_copies(group, step):
        device = {"seq": peer(step)}
        if group == 0:
            return [
                remote(source, target.at[seq], dec_send.at[which, step], dec_recv.at[which, seq], device)
                for which, source, target in ((0, dk, dkb), (1, dv, dvb))
            ]
        return [
            remote(source, target.at[seq], enc_send.at[which, step], enc_recv.at[which, seq], device)
            for which, source, target in ((0, ek, ekb), (1, ev, evb))
        ]

    def start_seq(group, step):
        for copy in seq_copies(group, step):
            copy.start()

    def end_seq(step):
        for copy in seq_copies(0, step) + seq_copies(1, step):
            copy.wait_send()

    each(1, n, functools.partial(start_seq, 0))
    w_copies = [
        remote(weight.at[:, columns(half, 1 - core)], w_v.at[half, pl.ds(depth, depth)],
               w_send.at[half], w_recv.at[half], {"sect": near})
        for half in range(2)
    ]
    for copy in w_copies:
        copy.start()

    enc_limit = lengths[sect]
    pairs = enc_width // PAIR

    def enc_chunk(source, first):
        landed(ekb.at[source], enc_recv.at[0, source])
        landed(evb.at[source], enc_recv.at[1, source])
        position = source * enc_rows + lax.broadcasted_iota(jnp.int32, (1, enc_rows), 1)
        bias = jnp.where(position < enc_limit, 0.0, LOW)
        for pair in range(pairs):
            lanes = pl.ds(pair * PAIR, PAIR)
            summed, high = attend(
                stack_heads(q_v[:, lanes]), ekb[source, :, lanes], evb[source, :, lanes], bias
            )
            if first:
                acc[pair] = summed
                highs[pair] = jnp.broadcast_to(high, highs.shape[1:])
            else:
                before = highs[pair][:, :1]
                top = jnp.maximum(before, high)
                acc[pair] = acc[pair] * jnp.exp2(before - top) + summed * jnp.exp2(high - top)
                highs[pair] = jnp.broadcast_to(top, highs.shape[1:])

    loads[0].wait()
    enc_chunk(seq, True)

    loads[1].wait()

    def cross_landed(source):
        landed(xkb.at[source], x_recv.at[0, source])
        landed(xvb.at[source], x_recv.at[1, source])

    each(0, n, cross_landed)
    each(1, n, functools.partial(start_seq, 1))
    length = n * enc_rows
    position = lax.broadcasted_iota(jnp.int32, (1, length), 1)
    bias = jnp.where(position < lengths[0], 0.0, LOW)
    summed, _ = attend(
        stack_heads(cq_v[...]), xkb[...].reshape(length, PAIR), xvb[...].reshape(length, PAIR), bias
    )
    ctx[...] = merge_heads(summed)
    ctx_copy = remote(ctx, ctx_in, ctx_send, ctx_recv, {"sect": near})
    ctx_copy.start()

    for load in w_loads:
        load.wait()
    for copy in w_copies:
        copy.wait_recv()
    ctx_copy.wait_recv()
    both = jnp.concatenate([ctx[...], ctx_in[...]], axis=1)
    order = list(range(1, mps)) + [0]

    def project(half, step):
        owner = lax.rem(mp + step, mps)
        lanes = pl.ds(pl.multiple_of(owner * block, block), block)
        return jnp.dot(both, w_v[half, :, lanes], preferred_element_type=F32)

    y_copies = {}
    for step in order:
        y_out[step] = project(1 - level, step).astype(BF16)
        y_copies[step] = remote(
            y_out.at[step], y_in.at[step], y_send.at[step], y_recv.at[step], {"sect": far}
        )
        y_copies[step].start()
    for step in order:
        own[step] = project(level, step)

    loads[2].wait()

    def dec_landed(source):
        landed(dkb.at[source], dec_recv.at[0, source])
        landed(dvb.at[source], dec_recv.at[1, source])

    each(0, n, dec_landed)
    length = n * dec_rows
    row = lax.broadcasted_iota(jnp.int32, (2 * dec_rows, length), 0)
    row = jnp.where(row >= dec_rows, row - dec_rows, row) + seq * dec_rows
    position = lax.broadcasted_iota(jnp.int32, (2 * dec_rows, length), 1)
    bias = jnp.where(position <= row, 0.0, LOW)
    summed, _ = attend(
        stack_heads(dq_v[...]), dkb[...].reshape(length, PAIR), dvb[...].reshape(length, PAIR), bias
    )
    self_out[...] = merge_heads(summed)

    z_copies = {}
    for step in range(1, mps):
        y_copies[step].wait_recv()
        z_out[step] = (own[step] + y_in[step].astype(F32)).astype(BF16)
        z_copies[step] = remote(
            z_out.at[step], z_in.at[step], z_send.at[step], z_recv.at[step],
            {"mp": lax.rem(mp + step, mps)},
        )
        z_copies[step].start()
    each(1, n, lambda step: enc_chunk(peer(step), False))
    for pair in range(pairs):
        enc_out[:, pair * PAIR:(pair + 1) * PAIR] = merge_heads(acc[pair])

    loads[3].wait()
    y_copies[0].wait_recv()
    total = own[0] + y_in[0].astype(F32)
    for step in range(1, mps):
        z_copies[step].wait_recv()
        total = total + z_in[step].astype(F32)
    dec_out[...] = (hid_v[...].astype(F32) + total).astype(BF16)

    @pl.when(sect == 0)
    def _():
        all_cross(end_cross)

    each(1, n, end_seq)
    for copy in w_copies + [ctx_copy] + list(y_copies.values()) + list(z_copies.values()):
        copy.wait_send()


def store(*refs):
    sources, targets, sems = refs[:3], refs[3:6], refs[6]
    copies = [
        pltpu.make_async_copy(source, target, sems.at[which])
        for which, (source, target) in enumerate(zip(sources, targets))
    ]
    for copy in copies:
        copy.start()
    for copy in copies:
        copy.wait()


def per_device(
    n, mps, enc_query, enc_keys, enc_values, enc_lengths, cross_keys, cross_values,
    cross_query, dec_query, dec_keys, dec_values, cross_out_weight, dec_hidden,
):
    enc_rows, enc_width = enc_query.shape[1:]
    dec_rows, _, narrow = cross_query.shape
    depth, model = cross_out_weight.shape[1:]
    block = dec_hidden.shape[1]
    span = model // SECTIONS
    pairs = enc_width // PAIR
    vmem, dma = pltpu.VMEM, pltpu.SemaphoreType.DMA
    in_hbm = pl.BlockSpec(memory_space=pltpu.HBM)
    in_vmem = pl.BlockSpec(memory_space=pltpu.VMEM)
    shapes = ((enc_rows, enc_width), (dec_rows, narrow), (dec_rows, block))
    results = pl.pallas_call(
        functools.partial(kernel, n, mps),
        out_shape=tuple(vmem(shape, BF16) for shape in shapes),
        in_specs=[in_hbm] * 3
        + [pl.BlockSpec(memory_space=pltpu.SMEM)]
        + [in_hbm] * 8,
        out_specs=(in_vmem,) * 3,
        scratch_shapes=[
            vmem((enc_rows, enc_width), BF16),
            vmem((n, enc_rows, enc_width), BF16),
            vmem((n, enc_rows, enc_width), BF16),
            vmem((n, enc_rows, narrow), BF16),
            vmem((n, enc_rows, narrow), BF16),
            vmem((dec_rows, narrow), BF16),
            vmem((dec_rows, narrow), BF16),
            vmem((n, dec_rows, narrow), BF16),
            vmem((n, dec_rows, narrow), BF16),
            vmem((2, 2 * depth, span), BF16),
            vmem((dec_rows, block), BF16),
            vmem((pairs, 2 * enc_rows, 2 * PAIR), F32),
            vmem((pairs, 2 * enc_rows, PAIR), F32),
            vmem((dec_rows, narrow), BF16),
            vmem((dec_rows, narrow), BF16),
            vmem((mps, dec_rows, block), BF16),
            vmem((mps, dec_rows, block), BF16),
            vmem((mps, dec_rows, block), F32),
            vmem((mps, dec_rows, block), BF16),
            vmem((mps, dec_rows, block), BF16),
            dma((4,)),
            dma((2, n)), dma((2, n)),
            dma((2, SECTIONS, n)), dma((2, n)),
            dma((2, n)), dma((2, n)),
            dma((2,)), dma((2,)), dma((2,)),
            dma, dma,
            dma((mps,)), dma((mps,)), dma((mps,)), dma((mps,)),
        ],
        compiler_params=pltpu.CompilerParams(
            collective_id=0, has_side_effects=True,
            vmem_limit_bytes=60 << 20,
        ),
    )(
        enc_query[0], enc_keys[0], enc_values[0], enc_lengths, cross_keys[0], cross_values[0],
        cross_query[:, 0, :], dec_query[:, 0, :], dec_keys[:, 0, :], dec_values[:, 0, :],
        cross_out_weight[0], dec_hidden,
    )
    enc_out, self_out, decoded = pl.pallas_call(
        store,
        out_shape=tuple(jax.ShapeDtypeStruct(shape, BF16) for shape in shapes),
        in_specs=[in_vmem] * 3,
        out_specs=(in_hbm,) * 3,
        scratch_shapes=[dma((3,))],
        compiler_params=pltpu.CompilerParams(vmem_limit_bytes=1 << 20),
    )(*results)
    return enc_out[None], self_out[:, None, :], decoded


def solution(mesh):
    in_specs = (
        P("sect", "seq", "mp"),
        P("sect", "seq", "mp"),
        P("sect", "seq", "mp"),
        P(),
        P("sect", "seq", "mp"),
        P("sect", "seq", "mp"),
        P("seq", "mp", "sect"),
        P("seq", "mp", "sect"),
        P("seq", "mp", "sect"),
        P("seq", "mp", "sect"),
        P("mp", "sect", None),
        P("seq", ("sect", "mp")),
    )
    out_specs = (P("sect", "seq", "mp"), P("seq", "mp", "sect"), P("seq", ("sect", "mp")))
    return jax.shard_map(
        functools.partial(per_device, mesh.shape["seq"], mesh.shape["mp"]),
        mesh=mesh, in_specs=in_specs, out_specs=out_specs, check_vma=False,
    )
```

```python
import functools
import math

import jax
import jax.numpy as jnp
from jax import lax
from jax.experimental import pallas as pl
from jax.experimental.pallas import tpu as pltpu
from jax.sharding import PartitionSpec as P

HEAD_DIM = 64
PAIR = 2 * HEAD_DIM
FACTOR = HEAD_DIM ** (-0.5) * math.log2(math.e)
LOW = -1e30
SECTIONS = 4
F32 = jnp.float32
BF16 = jnp.bfloat16


def each(low, high, body):
    if high - low <= 4:
        for step in range(low, high):
            body(step)
    else:
        lax.fori_loop(low, high, lambda step, carry: (body(step), carry)[1], 0)


def stack_heads(queries):
    lane = lax.broadcasted_iota(jnp.int32, queries.shape, 1)
    wide = queries.astype(F32)
    first = jnp.where(lane < HEAD_DIM, wide, 0.0).astype(BF16)
    second = jnp.where(lane < HEAD_DIM, 0.0, wide).astype(BF16)
    return jnp.concatenate([first, second], axis=0)


def attend(stacked, keys, values, bias):
    scores = lax.dot_general(stacked, keys, (((1,), (1,)), ((), ())), preferred_element_type=F32)
    scores = scores * FACTOR + bias
    high = jnp.max(scores, axis=1, keepdims=True)
    weights = jnp.exp2(scores - high).astype(BF16)
    wide = jnp.concatenate([values, jnp.ones_like(values)], axis=1)
    return jnp.dot(weights, wide, preferred_element_type=F32), high


def merge_heads(summed):
    context = summed[:, :PAIR] / summed[:, PAIR:]
    rows = context.shape[0] // 2
    lane = lax.broadcasted_iota(jnp.int32, (rows, PAIR), 1)
    return jnp.where(lane < HEAD_DIM, context[:rows], context[rows:]).astype(BF16)


def kernel(
    n, mps,
    eq, ek, ev, lengths, ck, cv, cq, dq, dk, dv, weight, hidden,
    enc_out, self_out, dec_out,
    q_v, ekb, evb, xkb, xvb, cq_v, dq_v, dkb, dvb, w_v, hid_v,
    acc, highs, ctx, ctx_in, y_out, y_in, own, z_out, z_in,
    load_sem, enc_send, enc_recv, x_send, x_recv, dec_send, dec_recv,
    w_send, w_recv, w_load, ctx_send, ctx_recv, y_send, y_recv, z_send, z_recv,
):
    seq, sect, mp = lax.axis_index("seq"), lax.axis_index("sect"), lax.axis_index("mp")
    enc_rows, enc_width = q_v.shape
    dec_rows = cq_v.shape[0]
    block = hid_v.shape[1]
    span = mps * block
    near = sect + 1 - 2 * lax.rem(sect, 2)
    far = lax.rem(sect + 2, SECTIONS)
    core = lax.rem(sect, 2)
    level = sect // 2
    MESH = pl.DeviceIdType.MESH

    def remote(source, target, send, recv, device):
        return pltpu.make_async_remote_copy(
            src_ref=source, dst_ref=target, send_sem=send, recv_sem=recv,
            device_id=device, device_id_type=MESH,
        )

    def peer(step):
        return lax.rem(seq + step, n)

    def landed(ref, sem):
        pltpu.make_async_copy(ref, ref, sem).wait()

    loads = [
        pltpu.make_async_copy(eq, q_v, load_sem.at[0]),
        pltpu.make_async_copy(cq, cq_v, load_sem.at[1]),
        pltpu.make_async_copy(dq, dq_v, load_sem.at[2]),
        pltpu.make_async_copy(hidden, hid_v, load_sem.at[3]),
        pltpu.make_async_copy(ek, ekb.at[seq], enc_recv.at[0, seq]),
        pltpu.make_async_copy(ev, evb.at[seq], enc_recv.at[1, seq]),
        pltpu.make_async_copy(dk, dkb.at[seq], dec_recv.at[0, seq]),
        pltpu.make_async_copy(dv, dvb.at[seq], dec_recv.at[1, seq]),
    ]
    for load in loads:
        load.start()

    def columns(half, side):
        return pl.ds(pl.multiple_of((2 * half + side) * span, span), span)

    depth = weight.shape[0]
    w_loads = [
        pltpu.make_async_copy(
            weight.at[:, columns(half, core)], w_v.at[half, pl.ds(0, depth)], w_load.at[half]
        )
        for half in range(2)
    ]
    for load in w_loads:
        load.start()

    def first_columns(source):
        return source.at[:, pl.ds(0, PAIR)]

    @pl.when(sect == 0)
    def _():
        pltpu.make_async_copy(first_columns(ck), xkb.at[seq], x_recv.at[0, seq]).start()
        pltpu.make_async_copy(first_columns(cv), xvb.at[seq], x_recv.at[1, seq]).start()

    barrier = pltpu.get_barrier_semaphore()

    def greet(seq_step, sect_step):
        pl.semaphore_signal(
            barrier, inc=1,
            device_id={"seq": peer(seq_step), "sect": lax.rem(sect + sect_step, SECTIONS)},
            device_id_type=MESH,
        )

    for sect_step in range(SECTIONS):
        each(1 if sect_step == 0 else 0, n, lambda step: greet(step, sect_step))
    for step in range(1, mps):
        pl.semaphore_signal(
            barrier, inc=1, device_id={"mp": lax.rem(mp + step, mps)}, device_id_type=MESH
        )
    pl.semaphore_wait(barrier, n * SECTIONS - 1 + mps - 1)

    def cross_copies(step, section):
        device = {"seq": peer(step), "sect": section}
        lanes = pl.ds(section * PAIR, PAIR)
        return [
            remote(source.at[:, lanes], target.at[seq], x_send.at[which, section, step],
                   x_recv.at[which, seq], device)
            for which, source, target in ((0, ck, xkb), (1, cv, xvb))
        ]

    def start_cross(step, section):
        for copy in cross_copies(step, section):
            copy.start()

    def end_cross(step, section):
        for copy in cross_copies(step, section):
            copy.wait_send()

    def all_cross(action):
        for section in (2, 3, 1, 0):
            each(1 if section == 0 else 0, n, lambda step: action(step, section))

    @pl.when(sect == 0)
    def _():
        all_cross(start_cross)

    def seq_copies(group, step):
        device = {"seq": peer(step)}
        if group == 0:
            return [
                remote(source, target.at[seq], dec_send.at[which, step], dec_recv.at[which, seq], device)
                for which, source, target in ((0, dk, dkb), (1, dv, dvb))
            ]
        return [
            remote(source, target.at[seq], enc_send.at[which, step], enc_recv.at[which, seq], device)
            for which, source, target in ((0, ek, ekb), (1, ev, evb))
        ]

    def start_seq(group, step):
        for copy in seq_copies(group, step):
            copy.start()

    def end_seq(step):
        for copy in seq_copies(0, step) + seq_copies(1, step):
            copy.wait_send()

    each(1, n, functools.partial(start_seq, 0))
    w_copies = [
        remote(weight.at[:, columns(half, 1 - core)], w_v.at[half, pl.ds(depth, depth)],
               w_send.at[half], w_recv.at[half], {"sect": near})
        for half in range(2)
    ]
    for copy in w_copies:
        copy.start()

    @pl.when(level == 1)
    def _():
        each(1, n, functools.partial(start_seq, 1))

    enc_limit = lengths[sect]
    pairs = enc_width // PAIR

    def enc_chunk(source, first):
        landed(ekb.at[source], enc_recv.at[0, source])
        landed(evb.at[source], enc_recv.at[1, source])
        position = source * enc_rows + lax.broadcasted_iota(jnp.int32, (1, enc_rows), 1)
        bias = jnp.where(position < enc_limit, 0.0, LOW)
        for pair in range(pairs):
            lanes = pl.ds(pair * PAIR, PAIR)
            summed, high = attend(
                stack_heads(q_v[:, lanes]), ekb[source, :, lanes], evb[source, :, lanes], bias
            )
            if first:
                acc[pair] = summed
                highs[pair] = jnp.broadcast_to(high, highs.shape[1:])
            else:
                before = highs[pair][:, :1]
                top = jnp.maximum(before, high)
                acc[pair] = acc[pair] * jnp.exp2(before - top) + summed * jnp.exp2(high - top)
                highs[pair] = jnp.broadcast_to(top, highs.shape[1:])

    loads[0].wait()
    enc_chunk(seq, True)

    loads[1].wait()

    def cross_landed(source):
        landed(xkb.at[source], x_recv.at[0, source])
        landed(xvb.at[source], x_recv.at[1, source])

    each(0, n, cross_landed)

    @pl.when(level == 0)
    def _():
        each(1, n, functools.partial(start_seq, 1))

    length = n * enc_rows
    position = lax.broadcasted_iota(jnp.int32, (1, length), 1)
    bias = jnp.where(position < lengths[0], 0.0, LOW)
    summed, _ = attend(
        stack_heads(cq_v[...]), xkb[...].reshape(length, PAIR), xvb[...].reshape(length, PAIR), bias
    )
    ctx[...] = merge_heads(summed)
    ctx_copy = remote(ctx, ctx_in, ctx_send, ctx_recv, {"sect": near})
    ctx_copy.start()

    loads[2].wait()

    def dec_landed(source):
        landed(dkb.at[source], dec_recv.at[0, source])
        landed(dvb.at[source], dec_recv.at[1, source])

    each(0, n, dec_landed)
    length = n * dec_rows
    row = lax.broadcasted_iota(jnp.int32, (2 * dec_rows, length), 0)
    row = jnp.where(row >= dec_rows, row - dec_rows, row) + seq * dec_rows
    position = lax.broadcasted_iota(jnp.int32, (2 * dec_rows, length), 1)
    bias = jnp.where(position <= row, 0.0, LOW)
    summed, _ = attend(
        stack_heads(dq_v[...]), dkb[...].reshape(length, PAIR), dvb[...].reshape(length, PAIR), bias
    )
    self_out[...] = merge_heads(summed)

    for load in w_loads:
        load.wait()
    for copy in w_copies:
        copy.wait_recv()
    ctx_copy.wait_recv()
    both = jnp.concatenate([ctx[...], ctx_in[...]], axis=1)
    order = list(range(1, mps)) + [0]

    def project(half, step):
        owner = lax.rem(mp + step, mps)
        lanes = pl.ds(pl.multiple_of(owner * block, block), block)
        return jnp.dot(both, w_v[half, :, lanes], preferred_element_type=F32)

    y_copies = {}
    for step in order:
        y_out[step] = project(1 - level, step).astype(BF16)
        y_copies[step] = remote(
            y_out.at[step], y_in.at[step], y_send.at[step], y_recv.at[step], {"sect": far}
        )
        y_copies[step].start()
    for step in order:
        own[step] = project(level, step)

    z_copies = {}
    for step in range(1, mps):
        y_copies[step].wait_recv()
        z_out[step] = (own[step] + y_in[step].astype(F32)).astype(BF16)
        z_copies[step] = remote(
            z_out.at[step], z_in.at[step], z_send.at[step], z_recv.at[step],
            {"mp": lax.rem(mp + step, mps)},
        )
        z_copies[step].start()
    each(1, n, lambda step: enc_chunk(peer(step), False))
    for pair in range(pairs):
        enc_out[:, pair * PAIR:(pair + 1) * PAIR] = merge_heads(acc[pair])

    loads[3].wait()
    y_copies[0].wait_recv()
    total = own[0] + y_in[0].astype(F32)
    for step in range(1, mps):
        z_copies[step].wait_recv()
        total = total + z_in[step].astype(F32)
    dec_out[...] = (hid_v[...].astype(F32) + total).astype(BF16)

    @pl.when(sect == 0)
    def _():
        all_cross(end_cross)

    each(1, n, end_seq)
    for copy in w_copies + [ctx_copy] + list(y_copies.values()) + list(z_copies.values()):
        copy.wait_send()


def store(*refs):
    sources, targets, sems = refs[:3], refs[3:6], refs[6]
    copies = [
        pltpu.make_async_copy(source, target, sems.at[which])
        for which, (source, target) in enumerate(zip(sources, targets))
    ]
    for copy in copies:
        copy.start()
    for copy in copies:
        copy.wait()


def per_device(
    n, mps, enc_query, enc_keys, enc_values, enc_lengths, cross_keys, cross_values,
    cross_query, dec_query, dec_keys, dec_values, cross_out_weight, dec_hidden,
):
    enc_rows, enc_width = enc_query.shape[1:]
    dec_rows, _, narrow = cross_query.shape
    depth, model = cross_out_weight.shape[1:]
    block = dec_hidden.shape[1]
    span = model // SECTIONS
    pairs = enc_width // PAIR
    vmem, dma = pltpu.VMEM, pltpu.SemaphoreType.DMA
    in_hbm = pl.BlockSpec(memory_space=pltpu.HBM)
    in_vmem = pl.BlockSpec(memory_space=pltpu.VMEM)
    shapes = ((enc_rows, enc_width), (dec_rows, narrow), (dec_rows, block))
    results = pl.pallas_call(
        functools.partial(kernel, n, mps),
        out_shape=tuple(vmem(shape, BF16) for shape in shapes),
        in_specs=[in_hbm] * 3
        + [pl.BlockSpec(memory_space=pltpu.SMEM)]
        + [in_hbm] * 8,
        out_specs=(in_vmem,) * 3,
        scratch_shapes=[
            vmem((enc_rows, enc_width), BF16),
            vmem((n, enc_rows, enc_width), BF16),
            vmem((n, enc_rows, enc_width), BF16),
            vmem((n, enc_rows, narrow), BF16),
            vmem((n, enc_rows, narrow), BF16),
            vmem((dec_rows, narrow), BF16),
            vmem((dec_rows, narrow), BF16),
            vmem((n, dec_rows, narrow), BF16),
            vmem((n, dec_rows, narrow), BF16),
            vmem((2, 2 * depth, span), BF16),
            vmem((dec_rows, block), BF16),
            vmem((pairs, 2 * enc_rows, 2 * PAIR), F32),
            vmem((pairs, 2 * enc_rows, PAIR), F32),
            vmem((dec_rows, narrow), BF16),
            vmem((dec_rows, narrow), BF16),
            vmem((mps, dec_rows, block), BF16),
            vmem((mps, dec_rows, block), BF16),
            vmem((mps, dec_rows, block), F32),
            vmem((mps, dec_rows, block), BF16),
            vmem((mps, dec_rows, block), BF16),
            dma((4,)),
            dma((2, n)), dma((2, n)),
            dma((2, SECTIONS, n)), dma((2, n)),
            dma((2, n)), dma((2, n)),
            dma((2,)), dma((2,)), dma((2,)),
            dma, dma,
            dma((mps,)), dma((mps,)), dma((mps,)), dma((mps,)),
        ],
        compiler_params=pltpu.CompilerParams(
            collective_id=0, has_side_effects=True,
            vmem_limit_bytes=60 << 20,
        ),
    )(
        enc_query[0], enc_keys[0], enc_values[0], enc_lengths, cross_keys[0], cross_values[0],
        cross_query[:, 0, :], dec_query[:, 0, :], dec_keys[:, 0, :], dec_values[:, 0, :],
        cross_out_weight[0], dec_hidden,
    )
    enc_out, self_out, decoded = pl.pallas_call(
        store,
        out_shape=tuple(jax.ShapeDtypeStruct(shape, BF16) for shape in shapes),
        in_specs=[in_vmem] * 3,
        out_specs=(in_hbm,) * 3,
        scratch_shapes=[dma((3,))],
        compiler_params=pltpu.CompilerParams(vmem_limit_bytes=1 << 20),
    )(*results)
    return enc_out[None], self_out[:, None, :], decoded


def solution(mesh):
    in_specs = (
        P("sect", "seq", "mp"),
        P("sect", "seq", "mp"),
        P("sect", "seq", "mp"),
        P(),
        P("sect", "seq", "mp"),
        P("sect", "seq", "mp"),
        P("seq", "mp", "sect"),
        P("seq", "mp", "sect"),
        P("seq", "mp", "sect"),
        P("seq", "mp", "sect"),
        P("mp", "sect", None),
        P("seq", ("sect", "mp")),
    )
    out_specs = (P("sect", "seq", "mp"), P("seq", "mp", "sect"), P("seq", ("sect", "mp")))
    return jax.shard_map(
        functools.partial(per_device, mesh.shape["seq"], mesh.shape["mp"]),
        mesh=mesh, in_specs=in_specs, out_specs=out_specs, check_vma=False,
    )
```
